256 devices in a mesh: row: 16 (over x_lo, z), col: 16 (over y, x_hi, core).
Axes of the slice: x: 4 (x_hi: 2, x_lo: 2; x = x_hi * 2 + x_lo), y: 4, z: 8, core: 2. Of those that a mesh axis runs over, the one named last changes fastest.
Arguments:
- grad_out: bfloat16 [512, 12288], P('row', 'col'), may hold values from -6 to 6
- pre_act: bfloat16 [512, 49152], P(None, 'row'), may hold values from -6 to 6
- weight: bfloat16 [49152, 12288], P('row', 'col'), may hold values from -0.02734375 to 0.02734375
Outputs:
- grad_pre: bfloat16 [512, 49152], P('col', 'row')
- grad_weight: bfloat16 [49152, 12288], P('row', 'col')
The draws below stay inside these ranges and needn't reach their ends.
All inputs are finite; a program needn't handle non-finite values.
Results may differ from the reference program's by a relative error of at most 0.022.
Values may be sent and summed in bfloat16 or wider, within the bound.
A program may use at most 64 MiB of HBM per device.

```python
import jax
import jax.numpy as jnp
from jax import lax

D = 12288
FF = 49152
TOK = 512
D_BLOCK = 768
N_COL = 16


def block_levels(key, extent, shards, least, high):
    def one(dim, blocks):
        steps = jax.random.uniform(jax.random.fold_in(jax.random.fold_in(key, 6), dim), (blocks,), jnp.float32, least / len(shards), high / len(shards))
        return jnp.repeat(jnp.exp(steps), extent[dim] // blocks).reshape((-1,) + (1,) * (len(extent) - dim - 1))

    factor_of = one(*shards[0])
    for cut in shards[1:]:
        factor_of = factor_of * one(*cut)
    return factor_of


def bell_draw(key, dims, deviation, limit, split=(), held_as=jnp.bfloat16):
    array = deviation * jax.random.normal(key, dims, jnp.float32)
    if split:
        array = array * block_levels(key, dims, split, -0.22, 0.18)
    return jnp.clip(array, -limit, limit).astype(held_as)


def setup_inputs(seed: int = 0) -> dict:
    keys = jax.random.split(jax.random.key(seed), 4)
    grad_out = bell_draw(keys[0], (TOK, D), 1.0, 6.0, ((0, 16), (1, 16)))
    pre_act = bell_draw(keys[1], (TOK, FF), 1.0, 6.0, ((1, 16),))
    weight = bell_draw(keys[2], (FF, D), FF ** -0.5, 0.02734375, ((0, 16), (1, 16)))
    return {"grad_out": grad_out, "pre_act": pre_act, "weight": weight}


def gelu_value(values):
    inner = 0.7978845608 * (values + 0.044715 * values * values * values)
    return 0.5 * values * (1.0 + jnp.tanh(inner))


def gelu_slope(values):
    inner = 0.7978845608 * (values + 0.044715 * values * values * values)
    tanh_value = jnp.tanh(inner)
    return 0.5 * (1.0 + tanh_value) + 0.5 * values * (1.0 - tanh_value * tanh_value) * 0.7978845608 * (1.0 + 3.0 * 0.044715 * values * values)


def reference(grad_out, pre_act, weight):
    pre_float = pre_act.astype(jnp.float32)
    activation = gelu_value(pre_float).astype(jnp.bfloat16)
    out_float = grad_out.astype(jnp.float32)
    weight_float = weight.astype(jnp.float32)

    def add_block(index, summed):
        offset = (index * D_BLOCK).astype(jnp.int32)
        columns = lax.dynamic_slice_in_dim(out_float, offset, D_BLOCK, 1)
        weight_cols = lax.dynamic_slice_in_dim(weight_float, offset, D_BLOCK, 1)
        piece_sum = jnp.dot(columns, weight_cols.T).astype(jnp.bfloat16)
        piece_sum = lax.optimization_barrier(piece_sum)
        return summed + piece_sum.astype(jnp.float32)

    grad_act = lax.fori_loop(jnp.int32(0), jnp.int32(N_COL), add_block, jnp.zeros((TOK, FF), jnp.float32))
    grad_pre = (grad_act * gelu_slope(pre_float)).astype(jnp.bfloat16)
    grad_weight = jnp.dot(activation.T, grad_out, preferred_element_type=jnp.float32).astype(jnp.bfloat16)
    return grad_pre, grad_weight
```

```python
import jax
import jax.numpy as jnp
from jax import lax
from jax.experimental import pallas as pl
from jax.experimental.pallas import tpu as pltpu
from jax.sharding import PartitionSpec as P

MESH = pl.DeviceIdType.MESH
ROWS = 32
WIDTH = 768
HIDDEN = 3072
TOKENS = 512
PIECE = 512
HALVES = 2
HALF = HIDDEN // HALVES

BATCHES = (
    ((0, 0), (1, 0), (0, 3), (0, 5)),
    ((0, 2), (0, 6), (1, 3), (1, 5)),
    ((1, 2), (1, 6), (0, 1), (0, 7)),
    ((0, 4), (1, 4), (1, 1), (1, 7)),
)
SLOTS = tuple(slot for batch in BATCHES for slot in batch)
INDEX = {slot: i for i, slot in enumerate(SLOTS)}
SEND_ORDER = (3, 5, 2, 6, 4, 1, 7)


def gelu_value(values):
    inner = 0.7978845608 * (values + 0.044715 * values * values * values)
    return 0.5 * values * (1.0 + jnp.tanh(inner))


def gelu_slope(values):
    inner = 0.7978845608 * (values + 0.044715 * values * values * values)
    tanh_value = jnp.tanh(inner)
    return 0.5 * (1.0 + tanh_value) + 0.5 * values * (
        1.0 - tanh_value * tanh_value
    ) * 0.7978845608 * (1.0 + 3.0 * 0.044715 * values * values)


def kernel(
    grad_out, pre_act, weight, grad_pre, grad_weight,
    pre, wide, tiles, act, partial, from_core, pair_sum, arrived,
    load_sem, tile_send, tile_recv, forward_send, core_send, core_recv, sum_send, sum_recv,
):
    row, col = lax.axis_index("row"), lax.axis_index("col")
    x_lo, z = row // 8, row % 8
    chip, core = col // 2, col % 2

    def at_z(distance):
        return x_lo * 8 + (z + distance) % 8

    def token_tile(slot):
        other, distance = slot
        return ((x_lo + other) % 2) * 8 + (z + distance) % 8

    def tile_rows(slot):
        return pl.ds(INDEX[slot] * ROWS, ROWS)

    partner_row = (row + 8) % 16
    partner_core = chip * 2 + 1 - core
    pair = (z + core) % 2

    own_load = pltpu.make_async_copy(grad_out, tiles.at[tile_rows((0, 0))], load_sem.at[0])
    own_load.start()
    pre_load = pltpu.make_async_copy(pre_act, pre, load_sem.at[1])
    pre_load.start()
    weight_load = pltpu.make_async_copy(weight, wide, load_sem.at[2])
    weight_load.start()

    barrier = pltpu.get_barrier_semaphore()
    for distance in SEND_ORDER:
        pl.semaphore_signal(barrier, inc=1, device_id=(at_z(distance), col), device_id_type=MESH)
    pl.semaphore_signal(barrier, inc=1, device_id=(partner_row, col), device_id_type=MESH)
    pl.semaphore_signal(barrier, inc=1, device_id=(row, partner_core), device_id_type=MESH)
    for step in range(1, 8):
        pl.semaphore_signal(
            barrier, inc=1, device_id=(row, ((chip + step) % 8) * 2 + core), device_id_type=MESH
        )
    own_load.wait()
    pl.semaphore_wait(barrier, 16)

    sends = []

    def send_tile(source_slot, landing_slot, send_sem, device_row):
        copy = pltpu.make_async_remote_copy(
            src_ref=tiles.at[tile_rows(source_slot)],
            dst_ref=tiles.at[tile_rows(landing_slot)],
            send_sem=send_sem,
            recv_sem=tile_recv.at[INDEX[landing_slot]],
            device_id=(device_row, col),
            device_id_type=MESH,
        )
        copy.start()
        sends.append(copy)

    send_tile((0, 0), (1, 0), forward_send.at[0], partner_row)
    for distance in SEND_ORDER:
        send_tile((0, 0), (0, (8 - distance) % 8), tile_send.at[distance], at_z(distance))

    def wait_tile(slot):
        pltpu.make_async_remote_copy(
            src_ref=tiles.at[tile_rows(slot)],
            dst_ref=tiles.at[tile_rows(slot)],
            send_sem=forward_send.at[0],
            recv_sem=tile_recv.at[INDEX[slot]],
            device_id=(partner_row, col),
            device_id_type=MESH,
        ).wait_recv()

    def take_and_forward(distance):
        wait_tile((0, distance))
        send_tile((0, distance), (1, distance), forward_send.at[distance], partner_row)

    def activate(slot):
        start = pl.multiple_of(token_tile(slot) * ROWS, ROWS)
        base = INDEX[slot] * ROWS

        def step(i, carry):
            offset = pl.multiple_of(i * 16, 16)
            values = pre[pl.ds(start + offset, 16), :].astype(jnp.float32)
            act[pl.ds(base + offset, 16), :] = gelu_value(values).astype(jnp.bfloat16)
            return carry

        lax.fori_loop(0, ROWS // 16, step, 0)

    def partial_half(batch, half):
        rows = pl.ds(batch * 4 * ROWS, 4 * ROWS)

        def step(i, carry):
            offset = pl.multiple_of(half * HALF + i * PIECE, PIECE)
            product = lax.dot_general(
                tiles[rows, :], wide[pl.ds(offset, PIECE), :], (((1,), (1,)), ((), ())),
                preferred_element_type=jnp.float32,
            )
            partial[rows, pl.ds(offset, PIECE)] = product.astype(jnp.bfloat16)
            return carry

        lax.fori_loop(0, HALF // PIECE, step, 0)

    def core_copy(batch, half):
        theirs = pl.multiple_of(batch * 4 * ROWS + (1 - pair) * 2 * ROWS, 2 * ROWS)
        columns = pl.ds(half * HALF, HALF)
        return pltpu.make_async_remote_copy(
            src_ref=partial.at[pl.ds(theirs, 2 * ROWS), columns],
            dst_ref=from_core.at[batch, :, columns],
            send_sem=core_send.at[batch, half],
            recv_sem=core_recv.at[batch, half],
            device_id=(row, partner_core),
            device_id_type=MESH,
        )

    def add_cores(batch, half):
        mine = pl.multiple_of(batch * 4 * ROWS + pair * 2 * ROWS, 2 * ROWS)
        columns = pl.ds(half * HALF, HALF)

        def step(i, carry):
            offset = pl.multiple_of(i * 16, 16)
            total = partial[pl.ds(mine + offset, 16), columns].astype(jnp.float32)
            total += from_core[batch, pl.ds(offset, 16), columns].astype(jnp.float32)
            pair_sum[batch, pl.ds(offset, 16), columns] = total.astype(jnp.bfloat16)
            return carry

        lax.fori_loop(0, 2 * ROWS // 16, step, 0)

    def owner_of(batch, index):
        even = token_tile(BATCHES[batch][index])
        odd = token_tile(BATCHES[batch][2 + index])
        return jnp.where(pair == 0, even, odd)

    def sum_copy(batch, index):
        owner = owner_of(batch, index)
        place = (chip - owner // 2 + 8) % 8 - 1
        place = jnp.maximum(place, 0)
        copy = pltpu.make_async_remote_copy(
            src_ref=pair_sum.at[batch, pl.ds(index * ROWS, ROWS)],
            dst_ref=arrived.at[place],
            send_sem=sum_send.at[batch, index],
            recv_sem=sum_recv.at[place],
            device_id=(row, owner),
            device_id_type=MESH,
        )
        return owner, copy

    pre_load.wait()
    take_and_forward(3)
    take_and_forward(5)
    wait_tile((1, 0))
    weight_load.wait()
    for batch in range(4):
        if batch == 1:
            for distance in (2, 6, 4, 1, 7):
                take_and_forward(distance)
            wait_tile((1, 3))
            wait_tile((1, 5))
        elif batch == 2:
            wait_tile((1, 2))
            wait_tile((1, 6))
        elif batch == 3:
            for distance in (4, 1, 7):
                wait_tile((1, distance))
        for half in range(HALVES):
            partial_half(batch, half)
            core_copy(batch, half).start()
        for slot in BATCHES[batch]:
            activate(slot)
        for half in range(HALVES):
            core_copy(batch, half).wait_recv()
            add_cores(batch, half)
        for index in range(2):
            owner, copy = sum_copy(batch, index)

            @pl.when(owner != col)
            def _():
                copy.start()

    def weight_step(i, carry):
        offset = pl.multiple_of(i * PIECE, PIECE)
        product = lax.dot_general(
            act[:, pl.ds(offset, PIECE)], tiles[...], (((0,), (0,)), ((), ())),
            preferred_element_type=jnp.float32,
        )
        grad_weight[pl.ds(offset, PIECE), :] = product.astype(jnp.bfloat16)
        return carry

    lax.fori_loop(0, HIDDEN // PIECE, weight_step, 0)

    own_batch, own_index = jnp.int32(0), jnp.int32(0)
    for batch in range(4):
        for index in range(2):
            here = owner_of(batch, index) == col
            own_batch = jnp.where(here, batch, own_batch)
            own_index = jnp.where(here, index, own_index)

    for place in range(7):
        pltpu.make_async_remote_copy(
            src_ref=arrived.at[place],
            dst_ref=arrived.at[place],
            send_sem=sum_send.at[0, 0],
            recv_sem=sum_recv.at[place],
            device_id=(row, partner_core),
            device_id_type=MESH,
        ).wait_recv()

    def finish(i, carry):
        offset = pl.multiple_of(i * 16, 16)
        total = pair_sum[own_batch, pl.ds(pl.multiple_of(own_index * ROWS + offset, 16), 16), :].astype(jnp.float32)
        for place in range(7):
            total += arrived[place, pl.ds(offset, 16), :].astype(jnp.float32)
        values = pre[pl.ds(pl.multiple_of(col * ROWS + offset, 16), 16), :].astype(jnp.float32)
        grad_pre[pl.ds(offset, 16), :] = (total * gelu_slope(values)).astype(jnp.bfloat16)
        return carry

    lax.fori_loop(0, ROWS // 16, finish, 0)

    for copy in sends:
        copy.wait_send()
    for batch in range(4):
        for half in range(HALVES):
            core_copy(batch, half).wait_send()
        for index in range(2):
            owner, copy = sum_copy(batch, index)

            @pl.when(owner != col)
            def _():
                copy.wait_send()


def body(grad_out, pre_act, weight):
    bf16 = jnp.bfloat16
    hbm = pl.BlockSpec(memory_space=pltpu.HBM)
    vmem = pl.BlockSpec(memory_space=pltpu.VMEM)
    dma = pltpu.SemaphoreType.DMA
    return pl.pallas_call(
        kernel,
        out_shape=(
            jax.ShapeDtypeStruct((ROWS, HIDDEN), bf16),
            jax.ShapeDtypeStruct((HIDDEN, WIDTH), bf16),
        ),
        in_specs=[hbm, hbm, hbm],
        out_specs=(vmem, vmem),
        scratch_shapes=[
            pltpu.VMEM((TOKENS, HIDDEN), bf16),
            pltpu.VMEM((HIDDEN, WIDTH), bf16),
            pltpu.VMEM((TOKENS, WIDTH), bf16),
            pltpu.VMEM((TOKENS, HIDDEN), bf16),
            pltpu.VMEM((TOKENS, HIDDEN), bf16),
            pltpu.VMEM((4, 2 * ROWS, HIDDEN), bf16),
            pltpu.VMEM((4, 2 * ROWS, HIDDEN), bf16),
            pltpu.VMEM((7, ROWS, HIDDEN), bf16),
            dma((3,)),
            dma((8,)),
            dma((16,)),
            dma((8,)),
            dma((4, HALVES)),
            dma((4, HALVES)),
            dma((4, 2)),
            dma((7,)),
        ],
        compiler_params=pltpu.CompilerParams(
            collective_id=0, has_side_effects=True, vmem_limit_bytes=62 * 10**6
        ),
        name="all_in_one",
    )(grad_out, pre_act, weight)


def solution(mesh):
    placed = (P("row", "col"), P(None, "row"), P("row", "col"))
    return jax.shard_map(
        body,
        mesh=mesh,
        in_specs=placed,
        out_specs=(P("col", "row"), P("row", "col")),
        check_vma=False,
    )
```

```python
import jax
import jax.numpy as jnp
from jax import lax
from jax.experimental import pallas as pl
from jax.experimental.pallas import tpu as pltpu
from jax.sharding import PartitionSpec as P

MESH = pl.DeviceIdType.MESH
ROWS = 32
WIDTH = 768
HIDDEN = 3072
TOKENS = 512
HALF = HIDDEN // 2
FIRST, SECOND = pl.ds(0, HALF), pl.ds(HALF, HALF)

BATCHES = (
    ((0, 0), (1, 0), (0, 1), (0, 7)),
    ((0, 2), (0, 6), (1, 1), (1, 7)),
    ((1, 2), (1, 6), (0, 3), (0, 5)),
    ((0, 4), (1, 4), (1, 3), (1, 5)),
)
SLOTS = tuple(slot for batch in BATCHES for slot in batch)
INDEX = {slot: i for i, slot in enumerate(SLOTS)}


def gelu_value(values):
    inner = 0.7978845608 * (values + 0.044715 * values * values * values)
    return 0.5 * values * (1.0 + jnp.tanh(inner))


def gelu_slope(values):
    inner = 0.7978845608 * (values + 0.044715 * values * values * values)
    tanh_value = jnp.tanh(inner)
    return 0.5 * (1.0 + tanh_value) + 0.5 * values * (
        1.0 - tanh_value * tanh_value
    ) * 0.7978845608 * (1.0 + 3.0 * 0.044715 * values * values)


def kernel(
    grad_out, pre_act, weight, grad_pre, grad_weight,
    pre, wide, tiles, act, partial, from_core, pair_sum, xa, ya, yb, xb,
    load_sem, tile_send, tile_recv, core_send, core_recv,
    a_send, b_send, xa_recv, ya_recv, yb_recv, xb_send, xb_recv,
):
    row, col = lax.axis_index("row"), lax.axis_index("col")
    x_lo, z = row // 8, row % 8
    y, x_hi, core = col // 4, (col // 2) % 2, col % 2
    pair = (z + core) % 2

    def at_z(distance):
        return (x_lo * 8 + (z + distance) % 8, col)

    def at_y(there):
        return (row, there * 4 + x_hi * 2 + core)

    other_row = ((row + 8) % 16, col)
    other_core = (row, col + 1 - 2 * core)
    other_x = (row, col + 2 - 4 * x_hi)

    def token_tile(slot):
        other, distance = slot
        return ((x_lo + other) % 2) * 8 + (z + distance) % 8

    own_load = pltpu.make_async_copy(grad_out, tiles.at[pl.ds(0, ROWS)], load_sem.at[0])
    own_load.start()
    weight_load = pltpu.make_async_copy(weight, wide, load_sem.at[1])
    weight_load.start()
    pre_load = pltpu.make_async_copy(pre_act, pre, load_sem.at[2])
    pre_load.start()

    barrier = pltpu.get_barrier_semaphore()
    peers = [at_z(1), at_z(7), at_z(2), at_z(6), other_row, other_core, other_x]
    peers += [at_y((y + step) % 4) for step in (1, 2, 3)]
    for peer in peers:
        pl.semaphore_signal(barrier, inc=1, device_id=peer, device_id_type=MESH)
    own_load.wait()
    pl.semaphore_wait(barrier, len(peers))

    sends = []

    def remote(src, dst, send_sem, recv_sem, peer):
        return pltpu.make_async_remote_copy(
            src_ref=src, dst_ref=dst, send_sem=send_sem, recv_sem=recv_sem,
            device_id=peer, device_id_type=MESH,
        )

    def landed(dst, recv_sem):
        remote(dst, dst, tile_send.at[0], recv_sem, other_core).wait_recv()

    def part(slot, half=None):
        if half is None:
            return tiles.at[pl.ds(INDEX[slot] * ROWS, ROWS)]
        return tiles.at[pl.ds(INDEX[slot] * ROWS + half * 16, 16)]

    def tile_sem(slot, half):
        return tile_recv.at[INDEX[slot] if half != 1 else len(SLOTS)]

    def send_tile(source, landing, peer, half=None):
        copy = remote(
            part(source, half), part(landing, half), tile_send.at[len(sends)], tile_sem(landing, half), peer
        )
        copy.start()
        sends.append(copy)

    def wait_tile(slot, half=None):
        landed(part(slot, half), tile_sem(slot, half))

    def across(distance):
        send_tile((0, distance), (1, distance), other_row)

    def activate(slot):
        start = pl.multiple_of(token_tile(slot) * ROWS, ROWS)
        base = INDEX[slot] * ROWS

        def step(i, carry):
            offset = pl.multiple_of(i * 16, 16)
            values = pre[pl.ds(start + offset, 16), :].astype(jnp.float32)
            act[pl.ds(base + offset, 16), :] = gelu_value(values).astype(jnp.bfloat16)
            return carry

        lax.fori_loop(0, ROWS // 16, step, 0)

    def core_copy(batch, half):
        theirs = pl.multiple_of(batch * 4 * ROWS + (1 - pair) * 2 * ROWS, 2 * ROWS)
        columns = pl.ds(half * HALF, HALF)
        return remote(
            partial.at[pl.ds(theirs, 2 * ROWS), columns], from_core.at[batch, :, columns],
            core_send.at[batch, half], core_recv.at[batch, half], other_core,
        )

    def multiply(batch, half):
        rows = pl.ds(batch * 4 * ROWS, 4 * ROWS)
        columns = pl.ds(half * HALF, HALF)
        product = lax.dot_general(
            tiles[rows, :], wide[columns, :], (((1,), (1,)), ((), ())),
            preferred_element_type=jnp.float32,
        )
        partial[rows, columns] = product.astype(jnp.bfloat16)
        core_copy(batch, half).start()

    def add_cores(batch, half):
        mine = pl.multiple_of(batch * 4 * ROWS + pair * 2 * ROWS, 2 * ROWS)
        columns = pl.ds(half * HALF, HALF)
        landed(from_core.at[batch, :, columns], core_recv.at[batch, half])

        def step(i, carry):
            offset = pl.multiple_of(i * 16, 16)
            total = partial[pl.ds(mine + offset, 16), columns].astype(jnp.float32)
            total += from_core[batch, pl.ds(offset, 16), columns].astype(jnp.float32)
            pair_sum[batch, pl.ds(offset, 16), columns] = total.astype(jnp.bfloat16)
            return carry

        lax.fori_loop(0, 2 * ROWS // 16, step, 0)

    def owner_of(batch, index):
        even = token_tile(BATCHES[batch][index])
        odd = token_tile(BATCHES[batch][2 + index])
        return jnp.where(pair == 0, even, odd)

    def place_of(batch, index):
        owner = owner_of(batch, index)
        owner_y, owner_x = owner // 4, (owner // 2) % 2
        same_y, same_x = owner_y == y, owner_x == x_hi
        behind = jnp.maximum((y - owner_y + 4) % 4 - 1, 0)
        return owner_y, same_y, same_x, behind

    def x_first(batch, index):
        return remote(
            pair_sum.at[batch, pl.ds(index * ROWS, ROWS), FIRST], xa.at[batch, index],
            a_send.at[batch, index], xa_recv.at[batch, index], other_x,
        )

    def y_second(batch, index):
        owner_y, _, _, behind = place_of(batch, index)
        return remote(
            pair_sum.at[batch, pl.ds(index * ROWS, ROWS), FIRST], ya.at[behind],
            a_send.at[batch, index], ya_recv.at[behind], at_y(owner_y),
        )

    def y_first(batch, index):
        owner_y, _, same_x, behind = place_of(batch, index)
        side = jnp.where(same_x, 0, 1)
        return remote(
            pair_sum.at[batch, pl.ds(index * ROWS, ROWS), SECOND], yb.at[side, behind],
            b_send.at[batch, index], yb_recv.at[side, behind], at_y(owner_y),
        )

    def first_hops(batch, half):
        for index in range(2):
            _, same_y, same_x, _ = place_of(batch, index)
            if half == 0:

                @pl.when(jnp.logical_not(same_x))
                def _():
                    x_first(batch, index).start()

            else:

                @pl.when(jnp.logical_not(same_y))
                def _():
                    y_first(batch, index).start()

    def second_hops(batch):
        for index in range(2):
            _, same_y, same_x, _ = place_of(batch, index)

            @pl.when(same_x)
            def _():
                landed(xa.at[batch, index], xa_recv.at[batch, index])

                def step(i, carry):
                    offset = pl.multiple_of(i * 16, 16)
                    rows = pl.ds(index * ROWS + offset, 16)
                    total = pair_sum[batch, rows, FIRST].astype(jnp.float32)
                    total += xa[batch, index, pl.ds(offset, 16), :].astype(jnp.float32)
                    pair_sum[batch, rows, FIRST] = total.astype(jnp.bfloat16)
                    return carry

                lax.fori_loop(0, ROWS // 16, step, 0)

                @pl.when(jnp.logical_not(same_y))
                def _():
                    y_second(batch, index).start()

    def weight_part(half):
        columns = pl.ds(half * HALF, HALF)
        product = lax.dot_general(
            act[:, columns], tiles[...], (((0,), (0,)), ((), ())),
            preferred_element_type=jnp.float32,
        )
        grad_weight[columns, :] = product.astype(jnp.bfloat16)

    send_tile((0, 0), (1, 0), other_row)
    for distance in (1, 7, 2, 6):
        send_tile((0, 0), (0, 8 - distance), at_z(distance))
    pre_load.wait()
    for slot in SLOTS:
        activate(slot)
    wait_tile((0, 1))
    across(1)
    wait_tile((0, 7))
    across(7)
    wait_tile((1, 0))
    weight_load.wait()
    multiply(0, 0)
    wait_tile((0, 2))
    send_tile((0, 2), (0, 3), at_z(7))
    send_tile((0, 2), (0, 4), at_z(6), half=0)
    across(2)
    wait_tile((0, 6))
    send_tile((0, 6), (0, 5), at_z(1))
    send_tile((0, 6), (0, 4), at_z(2), half=1)
    across(6)
    multiply(0, 1)
    for half in range(2):
        add_cores(0, half)
        first_hops(0, half)

    wait_tile((1, 1))
    wait_tile((1, 7))
    multiply(1, 0)
    multiply(1, 1)
    wait_tile((0, 3))
    across(3)
    wait_tile((0, 5))
    across(5)
    wait_tile((0, 4), half=0)
    wait_tile((0, 4), half=1)
    across(4)
    for half in range(2):
        add_cores(1, half)
        first_hops(1, half)
    second_hops(0)

    wait_tile((1, 2))
    wait_tile((1, 6))
    multiply(2, 0)
    multiply(2, 1)
    for half in range(2):
        add_cores(2, half)
        first_hops(2, half)

    wait_tile((1, 3))
    wait_tile((1, 5))
    wait_tile((1, 4))
    multiply(3, 0)
    multiply(3, 1)
    second_hops(1)
    for half in range(2):
        add_cores(3, half)
        first_hops(3, half)
    second_hops(2)
    weight_part(0)
    second_hops(3)

    own_at, partner_at = jnp.int32(0), jnp.int32(0)
    for batch in range(4):
        for index in range(2):
            _, same_y, same_x, _ = place_of(batch, index)
            here = batch * 2 + index
            own_at = jnp.where(jnp.logical_and(same_y, same_x), here, own_at)
            partner_at = jnp.where(jnp.logical_and(same_y, jnp.logical_not(same_x)), here, partner_at)

    def held(at, offset, columns):
        start = pl.multiple_of((at % 2) * ROWS + offset, 16)
        return pair_sum[at // 2, pl.ds(start, 16), columns].astype(jnp.float32)

    for behind in range(3):
        landed(yb.at[1, behind], yb_recv.at[1, behind])

    def partner_step(i, carry):
        offset = pl.multiple_of(i * 16, 16)
        total = held(partner_at, offset, SECOND)
        for behind in range(3):
            total += yb[1, behind, pl.ds(offset, 16), :].astype(jnp.float32)
        xb[0, pl.ds(offset, 16), :] = total.astype(jnp.bfloat16)
        return carry

    lax.fori_loop(0, ROWS // 16, partner_step, 0)
    partner_copy = remote(xb.at[0], xb.at[1], xb_send.at[0], xb_recv.at[0], other_x)
    partner_copy.start()
    weight_part(1)

    for behind in range(3):
        landed(ya.at[behind], ya_recv.at[behind])
        landed(yb.at[0, behind], yb_recv.at[0, behind])

    def slope_at(offset, columns):
        start = pl.multiple_of(col * ROWS + offset, 16)
        return gelu_slope(pre[pl.ds(start, 16), columns].astype(jnp.float32))

    def first_step(i, carry):
        offset = pl.multiple_of(i * 16, 16)
        total = held(own_at, offset, FIRST)
        for behind in range(3):
            total += ya[behind, pl.ds(offset, 16), :].astype(jnp.float32)
        grad_pre[pl.ds(offset, 16), FIRST] = (total * slope_at(offset, FIRST)).astype(jnp.bfloat16)
        return carry

    lax.fori_loop(0, ROWS // 16, first_step, 0)
    landed(xb.at[1], xb_recv.at[0])

    def second_step(i, carry):
        offset = pl.multiple_of(i * 16, 16)
        total = held(own_at, offset, SECOND) + xb[1, pl.ds(offset, 16), :].astype(jnp.float32)
        for behind in range(3):
            total += yb[0, behind, pl.ds(offset, 16), :].astype(jnp.float32)
        grad_pre[pl.ds(offset, 16), SECOND] = (total * slope_at(offset, SECOND)).astype(jnp.bfloat16)
        return carry

    lax.fori_loop(0, ROWS // 16, second_step, 0)

    for copy in sends:
        copy.wait_send()
    partner_copy.wait_send()
    for batch in range(4):
        for half in range(2):
            core_copy(batch, half).wait_send()
        for index in range(2):
            _, same_y, same_x, _ = place_of(batch, index)

            @pl.when(jnp.logical_not(jnp.logical_and(same_x, same_y)))
            def _():
                x_first(batch, index).wait_send()

            @pl.when(jnp.logical_not(same_y))
            def _():
                y_first(batch, index).wait_send()


def write_out(grad_pre, grad_weight, grad_pre_out, grad_weight_out, sem):
    copies = [
        pltpu.make_async_copy(grad_weight, grad_weight_out, sem.at[0]),
        pltpu.make_async_copy(grad_pre, grad_pre_out, sem.at[1]),
    ]
    for copy in copies:
        copy.start()
    for copy in copies:
        copy.wait()


def body(grad_out, pre_act, weight):
    bf16 = jnp.bfloat16
    hbm = pl.BlockSpec(memory_space=pltpu.HBM)
    vmem = pl.BlockSpec(memory_space=pltpu.VMEM)
    dma = pltpu.SemaphoreType.DMA
    shapes = (
        jax.ShapeDtypeStruct((ROWS, HIDDEN), bf16),
        jax.ShapeDtypeStruct((HIDDEN, WIDTH), bf16),
    )
    held = (pltpu.VMEM((ROWS, HIDDEN), bf16), pltpu.VMEM((HIDDEN, WIDTH), bf16))
    args = [pltpu.with_memory_space_constraint(a, pltpu.HBM) for a in (grad_out, pre_act, weight)]
    grad_pre, grad_weight = pl.pallas_call(
        kernel,
        out_shape=held,
        in_specs=[hbm, hbm, hbm],
        out_specs=(vmem, vmem),
        scratch_shapes=[
            pltpu.VMEM((TOKENS, HIDDEN), bf16),
            pltpu.VMEM((HIDDEN, WIDTH), bf16),
            pltpu.VMEM((TOKENS, WIDTH), bf16),
            pltpu.VMEM((TOKENS, HIDDEN), bf16),
            pltpu.VMEM((TOKENS, HIDDEN), bf16),
            pltpu.VMEM((4, 2 * ROWS, HIDDEN), bf16),
            pltpu.VMEM((4, 2 * ROWS, HIDDEN), bf16),
            pltpu.VMEM((4, 2, ROWS, HALF), bf16),
            pltpu.VMEM((3, ROWS, HALF), bf16),
            pltpu.VMEM((2, 3, ROWS, HALF), bf16),
            pltpu.VMEM((2, ROWS, HALF), bf16),
            dma((3,)),
            dma((16,)),
            dma((17,)),
            dma((4, 2)),
            dma((4, 2)),
            dma((4, 2)),
            dma((4, 2)),
            dma((4, 2)),
            dma((3,)),
            dma((2, 3)),
            dma((1,)),
            dma((1,)),
        ],
        compiler_params=pltpu.CompilerParams(
            collective_id=0, has_side_effects=True, vmem_limit_bytes=40_000_000
        ),
        name="gather_multiply_sum",
    )(*args)
    return pl.pallas_call(
        write_out,
        out_shape=shapes,
        in_specs=[vmem, vmem],
        out_specs=(hbm, hbm),
        scratch_shapes=[dma((2,))],
        compiler_params=pltpu.CompilerParams(vmem_limit_bytes=2**20),
        name="write_out",
    )(
        pltpu.with_memory_space_constraint(grad_pre, pltpu.VMEM),
        pltpu.with_memory_space_constraint(grad_weight, pltpu.VMEM),
    )


def solution(mesh):
    placed = (P("row", "col"), P(None, "row"), P("row", "col"))
    return jax.shard_map(
        body,
        mesh=mesh,
        in_specs=placed,
        out_specs=(P("col", "row"), P("row", "col")),
        check_vma=False,
    )
```

```python
import jax
import jax.numpy as jnp
from jax import lax
from jax.experimental import pallas as pl
from jax.experimental.pallas import tpu as pltpu
from jax.sharding import PartitionSpec as P

MESH = pl.DeviceIdType.MESH
ROWS = 32
WIDTH = 768
HIDDEN = 3072
TOKENS = 512
WIDTHS = (1536, 1536)
PARTS = (pl.ds(0, WIDTHS[0]), pl.ds(WIDTHS[0], WIDTHS[1]))
FIRST, SECOND = PARTS

BATCHES = (
    (((0, 0), (1, 0)), ((0, 1), (1, 7))),
    (((0, 2), (1, 6)), ((1, 1), (0, 7))),
    (((1, 2), (0, 6)), ((0, 3), (1, 5))),
    (((0, 4), (1, 4)), ((1, 3), (0, 5))),
)
SLOTS = tuple(slot for batch in BATCHES for group in batch for slot in group)
INDEX = {slot: i for i, slot in enumerate(SLOTS)}


def gelu_value(values):
    inner = 0.7978845608 * (values + 0.044715 * values * values * values)
    return 0.5 * values * (1.0 + jnp.tanh(inner))


def gelu_slope(values):
    inner = 0.7978845608 * (values + 0.044715 * values * values * values)
    tanh_value = jnp.tanh(inner)
    return 0.5 * (1.0 + tanh_value) + 0.5 * values * (
        1.0 - tanh_value * tanh_value
    ) * 0.7978845608 * (1.0 + 3.0 * 0.044715 * values * values)


def kernel(
    grad_out, pre_act, weight, grad_pre, grad_weight,
    pre, wide, tiles, act, partial, from_core, pair_sum, xa, ya, yb, xb, slope,
    load_sem, tile_send, tile_recv, core_send, core_recv,
    a_send, b_send, xa_recv, ya_recv, yb_recv, xb_send, xb_recv, ready,
):
    row, col = lax.axis_index("row"), lax.axis_index("col")
    x_lo, z = row // 8, row % 8
    y, x_hi, core = col // 4, (col // 2) % 2, col % 2
    pair = (z + core) % 2

    def at_z(distance):
        return (x_lo * 8 + (z + distance) % 8, col)

    def diagonal(distance):
        return ((1 - x_lo) * 8 + (z + distance) % 8, col)

    def at_y(there):
        return (row, there * 4 + x_hi * 2 + core)

    other_row = ((row + 8) % 16, col)
    other_core = (row, col + 1 - 2 * core)
    other_x = (row, col + 2 - 4 * x_hi)

    def token_tile(slot):
        other, distance = slot
        return ((x_lo + other) % 2) * 8 + (z + distance) % 8

    own_load = pltpu.make_async_copy(grad_out, tiles.at[pl.ds(0, ROWS)], load_sem.at[0])
    own_load.start()
    pre_load = pltpu.make_async_copy(pre_act, pre, load_sem.at[2])
    pre_load.start()
    weight_load = pltpu.make_async_copy(weight, wide, load_sem.at[1])
    weight_load.start()

    barrier = pltpu.get_barrier_semaphore()
    peers = [at_z(d) for d in (1, 7, 2, 6)] + [diagonal(d) for d in (1, 7, 2, 6)]
    peers += [other_row, other_core]
    for peer in peers:
        pl.semaphore_signal(barrier, inc=1, device_id=peer, device_id_type=MESH)

    @pl.when(x_hi == 0)
    def _():
        pl.semaphore_signal(barrier, inc=1, device_id=other_x, device_id_type=MESH)

    for there in range(1, 4):

        @pl.when(there > y)
        def _():
            pl.semaphore_signal(barrier, inc=1, device_id=at_y(there), device_id_type=MESH)

    pl.semaphore_wait(barrier, len(peers) + x_hi + y)

    sends = []

    def remote(src, dst, send_sem, recv_sem, peer):
        return pltpu.make_async_remote_copy(
            src_ref=src, dst_ref=dst, send_sem=send_sem, recv_sem=recv_sem,
            device_id=peer, device_id_type=MESH,
        )

    def landed(dst, recv_sem):
        remote(dst, dst, tile_send.at[0], recv_sem, other_core).wait_recv()

    def part(slot):
        return tiles.at[pl.ds(INDEX[slot] * ROWS, ROWS)]

    def send_tile(source, landing, peer):
        copy = remote(
            grad_out if source == (0, 0) else part(source), part(landing),
            tile_send.at[len(sends)], tile_recv.at[INDEX[landing]], peer,
        )
        copy.start()
        sends.append(copy)

    def wait_tile(slot):
        landed(part(slot), tile_recv.at[INDEX[slot]])

    def across(slot):
        send_tile(slot, (1 - slot[0], slot[1]), other_row)

    def activate(slot):
        start = pl.multiple_of(token_tile(slot) * ROWS, ROWS)
        base = INDEX[slot] * ROWS

        def step(i, carry):
            offset = pl.multiple_of(i * 16, 16)
            values = pre[pl.ds(start + offset, 16), :].astype(jnp.float32)
            act[pl.ds(base + offset, 16), :] = gelu_value(values).astype(jnp.bfloat16)
            return carry

        lax.fori_loop(0, ROWS // 16, step, 0)

    def groups(batch):
        for parity, slots in enumerate(BATCHES[batch]):
            if slots:
                yield parity, slots, pl.ds(INDEX[slots[0]] * ROWS, len(slots) * ROWS)

    def core_copy(batch, parity, rows, part):
        return remote(
            partial.at[rows, PARTS[part]], from_core.at[rows, PARTS[part]],
            core_send.at[batch, parity, part], core_recv.at[batch, parity, part], other_core,
        )

    def multiply(batch, part):
        slots = BATCHES[batch][0] + BATCHES[batch][1]
        every = pl.ds(INDEX[slots[0]] * ROWS, len(slots) * ROWS)
        columns = PARTS[part]
        product = lax.dot_general(
            tiles[every, :], wide[columns, :], (((1,), (1,)), ((), ())),
            preferred_element_type=jnp.float32,
        )
        partial[every, columns] = product.astype(jnp.bfloat16)
        for parity, _, rows in groups(batch):

            @pl.when(pair != parity)
            def _():
                core_copy(batch, parity, rows, part).start()

    def place_of(slot):
        owner = token_tile(slot)
        owner_y, owner_x = owner // 4, (owner // 2) % 2
        same_y, same_x = owner_y == y, owner_x == x_hi
        behind = jnp.maximum((y - owner_y + 4) % 4 - 1, 0)
        return owner_y, same_y, same_x, behind

    def slot_rows(slot):
        return pl.ds(INDEX[slot] * ROWS, ROWS)

    def x_first(slot):
        i = INDEX[slot]
        return remote(
            pair_sum.at[slot_rows(slot), FIRST], xa.at[i], a_send.at[i], xa_recv.at[i], other_x
        )

    def y_second(slot):
        owner_y, _, _, behind = place_of(slot)
        return remote(
            pair_sum.at[slot_rows(slot), FIRST], ya.at[behind],
            a_send.at[INDEX[slot]], ya_recv.at[behind], at_y(owner_y),
        )

    def y_first(slot):
        owner_y, _, same_x, behind = place_of(slot)
        side = jnp.where(same_x, 0, 1)
        return remote(
            pair_sum.at[slot_rows(slot), SECOND], yb.at[side, behind],
            b_send.at[INDEX[slot]], yb_recv.at[side, behind], at_y(owner_y),
        )

    def first_hops(batch, part):
        columns = PARTS[part]
        for parity, slots, rows in groups(batch):

            @pl.when(pair == parity)
            def _():
                landed(from_core.at[rows, columns], core_recv.at[batch, parity, part])
                for slot in slots:

                    def step(i, carry):
                        at = pl.ds(pl.multiple_of(INDEX[slot] * ROWS + i * 16, 16), 16)
                        total = partial[at, columns].astype(jnp.float32)
                        total += from_core[at, columns].astype(jnp.float32)
                        pair_sum[at, columns] = total.astype(jnp.bfloat16)
                        return carry

                    lax.fori_loop(0, ROWS // 16, step, 0)
                    _, same_y, same_x, _ = place_of(slot)
                    if part == 0:

                        @pl.when(jnp.logical_not(same_x))
                        def _():
                            x_first(slot).start()

                    else:

                        @pl.when(jnp.logical_not(same_y))
                        def _():
                            y_first(slot).start()

    def second_hops(batch):
        for parity, slots, _ in groups(batch):
            for slot in slots:
                _, same_y, same_x, _ = place_of(slot)
                i = INDEX[slot]

                @pl.when(jnp.logical_and(pair == parity, same_x))
                def _():
                    landed(xa.at[i], xa_recv.at[i])

                    def step(j, carry):
                        offset = pl.multiple_of(j * 16, 16)
                        at = pl.ds(i * ROWS + offset, 16)
                        total = pair_sum[at, FIRST].astype(jnp.float32)
                        total += xa[i, pl.ds(offset, 16), :].astype(jnp.float32)
                        pair_sum[at, FIRST] = total.astype(jnp.bfloat16)
                        return carry

                    lax.fori_loop(0, ROWS // 16, step, 0)

                    @pl.when(jnp.logical_not(same_y))
                    def _():
                        y_second(slot).start()

    def find_slope():
        def step(i, carry):
            offset = pl.multiple_of(i * 16, 16)
            values = pre[pl.ds(pl.multiple_of(col * ROWS + offset, 16), 16), :].astype(jnp.float32)
            slope[pl.ds(offset, 16), :] = gelu_slope(values)
            return carry

        lax.fori_loop(0, ROWS // 16, step, 0)

    def weight_part(part):
        columns = PARTS[part]
        product = lax.dot_general(
            act[:, columns], tiles[...], (((0,), (0,)), ((), ())),
            preferred_element_type=jnp.float32,
        )
        grad_weight[columns, :] = product.astype(jnp.bfloat16)

    send_tile((0, 0), (1, 0), other_row)
    send_tile((0, 0), (0, 1), at_z(7))
    send_tile((0, 0), (1, 7), diagonal(1))
    send_tile((0, 0), (0, 2), at_z(6))
    send_tile((0, 0), (1, 6), diagonal(2))

    @pl.when(x_hi == 1)
    def _():
        pl.semaphore_signal(ready, inc=1, device_id=other_x, device_id_type=MESH)

    for there in range(3):

        @pl.when(there < y)
        def _():
            pl.semaphore_signal(ready, inc=1, device_id=at_y(there), device_id_type=MESH)

    pre_load.wait()
    for slot in SLOTS:
        activate(slot)
    for slot in ((0, 1), (1, 7)):
        wait_tile(slot)
        across(slot)
    own_load.wait()
    weight_load.wait()
    wait_tile((1, 0))
    multiply(0, 0)
    wait_tile((0, 2))
    send_tile((0, 2), (0, 3), at_z(7))
    send_tile((0, 2), (0, 4), at_z(6))
    across((0, 2))
    wait_tile((1, 6))
    send_tile((1, 6), (1, 5), at_z(1))
    send_tile((1, 6), (1, 4), at_z(2))
    across((1, 6))
    multiply(0, 1)
    find_slope()
    for count in range(1, 5):

        @pl.when(4 - x_hi - y == count)
        def _():
            pl.semaphore_wait(ready, count)

    first_hops(0, 0)
    first_hops(0, 1)

    for slot in ((1, 1), (0, 7)):
        wait_tile(slot)
    multiply(1, 0)
    multiply(1, 1)
    for slot in ((0, 3), (1, 5)):
        wait_tile(slot)
        across(slot)
    first_hops(1, 0)
    first_hops(1, 1)
    second_hops(0)

    for slot in ((1, 2), (0, 6)):
        wait_tile(slot)
    multiply(2, 0)
    multiply(2, 1)
    first_hops(2, 0)
    first_hops(2, 1)

    for slot in ((0, 4), (1, 4), (1, 3), (0, 5)):
        wait_tile(slot)
    multiply(3, 0)
    multiply(3, 1)
    second_hops(1)
    first_hops(3, 0)
    first_hops(3, 1)
    second_hops(2)
    weight_part(0)
    second_hops(3)

    own_at, partner_at = jnp.int32(0), jnp.int32(0)
    for slot in SLOTS:
        own_at = jnp.where(token_tile(slot) == col, INDEX[slot], own_at)
        partner_at = jnp.where(token_tile(slot) == other_x[1], INDEX[slot], partner_at)

    def held(at, offset, columns):
        start = pl.multiple_of(at * ROWS + offset, 16)
        return pair_sum[pl.ds(start, 16), columns].astype(jnp.float32)

    for behind in range(3):
        landed(yb.at[1, behind], yb_recv.at[1, behind])

    def partner_step(i, carry):
        offset = pl.multiple_of(i * 16, 16)
        total = held(partner_at, offset, SECOND)
        for behind in range(3):
            total += yb[1, behind, pl.ds(offset, 16), :].astype(jnp.float32)
        xb[0, pl.ds(offset, 16), :] = total.astype(jnp.bfloat16)
        return carry

    lax.fori_loop(0, ROWS // 16, partner_step, 0)
    partner_copy = remote(xb.at[0], xb.at[1], xb_send.at[0], xb_recv.at[0], other_x)
    partner_copy.start()
    weight_part(1)

    for behind in range(3):
        landed(ya.at[behind], ya_recv.at[behind])
        landed(yb.at[0, behind], yb_recv.at[0, behind])

    def first_step(i, carry):
        offset = pl.multiple_of(i * 16, 16)
        total = held(own_at, offset, FIRST)
        for behind in range(3):
            total += ya[behind, pl.ds(offset, 16), :].astype(jnp.float32)
        grad_pre[pl.ds(offset, 16), FIRST] = (total * slope[pl.ds(offset, 16), FIRST]).astype(jnp.bfloat16)
        return carry

    lax.fori_loop(0, ROWS // 16, first_step, 0)
    landed(xb.at[1], xb_recv.at[0])

    def second_step(i, carry):
        offset = pl.multiple_of(i * 16, 16)
        total = held(own_at, offset, SECOND) + xb[1, pl.ds(offset, 16), :].astype(jnp.float32)
        for behind in range(3):
            total += yb[0, behind, pl.ds(offset, 16), :].astype(jnp.float32)
        grad_pre[pl.ds(offset, 16), SECOND] = (total * slope[pl.ds(offset, 16), SECOND]).astype(jnp.bfloat16)
        return carry

    lax.fori_loop(0, ROWS // 16, second_step, 0)

    for copy in sends:
        copy.wait_send()
    partner_copy.wait_send()
    for batch in range(len(BATCHES)):
        for parity, slots, rows in groups(batch):

            @pl.when(pair != parity)
            def _():
                for part in range(2):
                    core_copy(batch, parity, rows, part).wait_send()

            for slot in slots:
                _, same_y, same_x, _ = place_of(slot)
                mine = pair == parity

                @pl.when(jnp.logical_and(mine, jnp.logical_not(jnp.logical_and(same_x, same_y))))
                def _():
                    x_first(slot).wait_send()

                @pl.when(jnp.logical_and(mine, jnp.logical_not(same_y)))
                def _():
                    y_first(slot).wait_send()


def write_out(grad_pre, grad_weight, grad_pre_out, grad_weight_out, sem):
    copies = [
        pltpu.make_async_copy(grad_weight, grad_weight_out, sem.at[0]),
        pltpu.make_async_copy(grad_pre, grad_pre_out, sem.at[1]),
    ]
    for copy in copies:
        copy.start()
    for copy in copies:
        copy.wait()


def body(grad_out, pre_act, weight):
    bf16 = jnp.bfloat16
    hbm = pl.BlockSpec(memory_space=pltpu.HBM)
    vmem = pl.BlockSpec(memory_space=pltpu.VMEM)
    dma = pltpu.SemaphoreType.DMA
    shapes = (
        jax.ShapeDtypeStruct((ROWS, HIDDEN), bf16),
        jax.ShapeDtypeStruct((HIDDEN, WIDTH), bf16),
    )
    held = (pltpu.VMEM((ROWS, HIDDEN), bf16), pltpu.VMEM((HIDDEN, WIDTH), bf16))
    args = [pltpu.with_memory_space_constraint(a, pltpu.HBM) for a in (grad_out, pre_act, weight)]
    grad_pre, grad_weight = pl.pallas_call(
        kernel,
        out_shape=held,
        in_specs=[hbm, hbm, hbm],
        out_specs=(vmem, vmem),
        scratch_shapes=[
            pltpu.VMEM((TOKENS, HIDDEN), bf16),
            pltpu.VMEM((HIDDEN, WIDTH), bf16),
            pltpu.VMEM((TOKENS, WIDTH), bf16),
            pltpu.VMEM((TOKENS, HIDDEN), bf16),
            pltpu.VMEM((TOKENS, HIDDEN), bf16),
            pltpu.VMEM((TOKENS, HIDDEN), bf16),
            pltpu.VMEM((TOKENS, HIDDEN), bf16),
            pltpu.VMEM((16, ROWS, WIDTHS[0]), bf16),
            pltpu.VMEM((3, ROWS, WIDTHS[0]), bf16),
            pltpu.VMEM((2, 3, ROWS, WIDTHS[1]), bf16),
            pltpu.VMEM((2, ROWS, WIDTHS[1]), bf16),
            pltpu.VMEM((ROWS, HIDDEN), jnp.float32),
            dma((3,)),
            dma((16,)),
            dma((16,)),
            dma((4, 2, 2)),
            dma((4, 2, 2)),
            dma((16,)),
            dma((16,)),
            dma((16,)),
            dma((3,)),
            dma((2, 3)),
            dma((1,)),
            dma((1,)),
            pltpu.SemaphoreType.REGULAR,
        ],
        compiler_params=pltpu.CompilerParams(
            collective_id=0, has_side_effects=True, vmem_limit_bytes=40_000_000
        ),
        name="gather_multiply_sum",
    )(*args)
    return pl.pallas_call(
        write_out,
        out_shape=shapes,
        in_specs=[vmem, vmem],
        out_specs=(hbm, hbm),
        scratch_shapes=[dma((2,))],
        compiler_params=pltpu.CompilerParams(vmem_limit_bytes=2**20),
        name="write_out",
    )(
        pltpu.with_memory_space_constraint(grad_pre, pltpu.VMEM),
        pltpu.with_memory_space_constraint(grad_weight, pltpu.VMEM),
    )


def solution(mesh):
    placed = (P("row", "col"), P(None, "row"), P("row", "col"))
    return jax.shard_map(
        body,
        mesh=mesh,
        in_specs=placed,
        out_specs=(P("col", "row"), P("row", "col")),
        check_vma=False,
    )
```
